32 devices in a mesh: ctx: 8 (over z, x), uly: 4 (over y, core).
Axes of the slice: x: 2, y: 2, z: 4, core: 2. Of those that a mesh axis runs over, the one named last changes fastest.
Arguments:
- q_new: bfloat16 [512, 4096], P(('ctx', 'uly')), may hold values from -20 to 20
- k_new: bfloat16 [512, 4096], P(('ctx', 'uly')), may hold values from -6 to 6
- v_new: bfloat16 [512, 4096], P(('ctx', 'uly')), may hold values from -6 to 6
- cache_k: bfloat16 [8192, 4096], P('ctx', 'uly'), may hold values from -4 to 4
- cache_v: bfloat16 [8192, 4096], P('ctx', 'uly'), may hold values from -6 to 6
- filled_slots: int32 [1], replicated, may hold values from 4097 to 8192
- norm_gain: float32 [4096], replicated, may hold values from 0.1 to 1.9
- v_branch: bfloat16 [512, 4096], P(('ctx', 'uly')), may hold values from -6 to 6
- x_gate: bfloat16 [512, 4096], P(('ctx', 'uly')), may hold values from -6 to 6
- conv_state: bfloat16 [6, 4096], replicated, may hold values from -6 to 6
- conv_filter: float32 [7, 256], replicated, may hold values from -2 to 2
- skip_gain: float32 [4096], replicated, may hold values from -1 to 1
Outputs:
- mixed: bfloat16 [512, 4096], P(('ctx', 'uly'))
The draws below stay inside these ranges and needn't reach their ends.
All inputs are finite; a program needn't handle non-finite values.
Results may differ from the reference program's by a relative error of at most 0.04.
Values may be sent and summed in bfloat16 or wider, within the bound.
No kernel may reach another device: no remote copies, remote signals or barrier semaphores. Data moves between devices by JAX's collectives and lax.ppermute only.
A program may use at most 128 MiB of HBM per device.

```python
import math
import jax
import jax.numpy as jnp
from jax import lax

D = 4096
HEADS = 32
DH = 128
CHAN_GROUP = 16
TAPS = 7
TOKENS = 512
CACHE = 8192
GROUPS = 256


def draw_q_new(key, part):
    base = jnp.clip(jax.random.normal(jax.random.fold_in(key, 11), (TOKENS, HEADS * DH), jnp.float32), -4.0, 4.0)
    return base.astype(jnp.bfloat16)


def draw_cache_k(key, part):
    base = jnp.clip(jax.random.normal(jax.random.fold_in(key, 21), (CACHE, HEADS * DH), jnp.float32), -4.0, 4.0)
    return base.astype(jnp.bfloat16)


def shard_levels(stream_key, dims, split, least, high):
    def one(axis_at, blocks):
        draws = jax.random.uniform(jax.random.fold_in(jax.random.fold_in(stream_key, 6), axis_at), (blocks,), jnp.float32, least / len(split), high / len(split))
        return jnp.repeat(jnp.exp(draws), dims[axis_at] // blocks).reshape((-1,) + (1,) * (len(dims) - axis_at - 1))

    level = one(*split[0])
    for cut in split[1:]:
        level = level * one(*cut)
    return level


def bell_draw(rng, dims, deviation, limit, pieces=(), kind=jnp.bfloat16):
    entries = deviation * jax.random.normal(rng, dims, jnp.float32)
    if pieces:
        entries = entries * shard_levels(rng, dims, pieces, -0.22, 0.18)
    return jnp.clip(entries, -limit, limit).astype(kind)


def setup_inputs(seed: int = 0) -> dict:
    splits = jax.random.split(jax.random.key(seed), 13)
    return {
        "q_new": draw_q_new(jax.random.fold_in(splits[12], 71), 0),
        "k_new": bell_draw(splits[1], (TOKENS, D), 1.0, 6.0, ((0, 32),)),
        "v_new": bell_draw(splits[2], (TOKENS, D), 1.0, 6.0, ((0, 32),)),
        "cache_k": draw_cache_k(jax.random.fold_in(splits[12], 71), 0),
        "cache_v": bell_draw(splits[4], (CACHE, D), 1.0, 6.0, ((0, 8), (1, 4))),
        "filled_slots": jax.random.randint(splits[5], (1,), CACHE // 2 + 1, CACHE + 1).astype(jnp.int32),
        "norm_gain": jnp.clip(1.0 + 0.18 * jax.random.normal(splits[6], (D,), jnp.float32), 0.1, 1.9),
        "v_branch": bell_draw(splits[7], (TOKENS, D), 1.0, 6.0, ((0, 32),)),
        "x_gate": bell_draw(splits[8], (TOKENS, D), 1.0, 6.0, ((0, 32),)),
        "conv_state": bell_draw(splits[9], (TAPS - 1, D), 1.0, 6.0),
        "conv_filter": bell_draw(splits[10], (TAPS, GROUPS), TAPS ** -0.5, 2.0, (), jnp.float32),
        "skip_gain": jnp.clip(jax.random.uniform(splits[11], (D,), jnp.float32, -1.0, 1.0), -1.0, 1.0),
    }


def reference(q_new, k_new, v_new, cache_k, cache_v, filled_slots, norm_gain, v_branch, x_gate, conv_state, conv_filter, skip_gain):
    cache_limit = filled_slots[0]
    all_keys = jnp.concatenate([cache_k, k_new], axis=0)
    all_values = jnp.concatenate([cache_v, v_new], axis=0)
    slot_ids = jnp.arange(all_keys.shape[0], dtype=jnp.int32)[None, :]
    score_scale = 1.0 / math.sqrt(DH)
    block_width = math.gcd(TOKENS, 1024)
    block_count = TOKENS // block_width

    def one_head(head_id):
        head_q = lax.dynamic_slice_in_dim(q_new, head_id * DH, DH, 1)
        head_k = lax.dynamic_slice_in_dim(all_keys, head_id * DH, DH, 1)
        head_v = lax.dynamic_slice_in_dim(all_values, head_id * DH, DH, 1)

        def one_block(block_id):
            queries = lax.dynamic_slice_in_dim(head_q, block_id * block_width, block_width, 0)
            positions = (block_id * block_width + jnp.arange(block_width, dtype=jnp.int32))[:, None]
            scores = jnp.dot(queries, head_k.T, preferred_element_type=jnp.float32) * score_scale
            valid_mask = jnp.where(slot_ids < CACHE, slot_ids < cache_limit, slot_ids - CACHE <= positions)
            scores = jnp.where(valid_mask, scores, -jnp.inf)
            largest = lax.optimization_barrier(jnp.max(scores, axis=1, keepdims=True))
            weights = jnp.exp(scores - largest)
            denominator = lax.optimization_barrier(jnp.sum(weights, axis=1, keepdims=True))
            numerator = jnp.dot(weights.astype(jnp.bfloat16), head_v, preferred_element_type=jnp.float32)
            return numerator / denominator
        return lax.map(one_block, jnp.arange(block_count, dtype=jnp.int32)).reshape(TOKENS, DH)
    per_head = lax.map(one_head, jnp.arange(HEADS, dtype=jnp.int32))
    attended = jnp.transpose(per_head, (1, 0, 2)).reshape(TOKENS, D).astype(jnp.bfloat16)
    values32 = attended.astype(jnp.float32)
    normed = values32 * lax.rsqrt(lax.optimization_barrier(jnp.mean(values32 * values32, axis=1, keepdims=True)) + 1e-06) * norm_gain
    conv_input = lax.optimization_barrier((normed * v_branch.astype(jnp.float32)).astype(jnp.bfloat16))
    extended = jnp.concatenate([conv_state, conv_input], axis=0).astype(jnp.float32)
    tap_table = jnp.repeat(conv_filter, CHAN_GROUP, axis=1)
    conv_reach = TAPS - 1
    filtered = tap_table[0] * extended[conv_reach:conv_reach + TOKENS]
    for shift_lag in range(1, TAPS):
        filtered = filtered + tap_table[shift_lag] * extended[conv_reach - shift_lag:conv_reach - shift_lag + TOKENS]
    result = x_gate.astype(jnp.float32) * (filtered + skip_gain * conv_input.astype(jnp.float32))
    return result.astype(jnp.bfloat16)
```

```python
import functools
import math

import jax
import jax.numpy as jnp
from jax import lax
from jax.experimental import pallas as pl
from jax.experimental.pallas import tpu as pltpu
from jax.sharding import PartitionSpec as P

DH = 128
MASKED = -(2.0**100)
EXP2_SCALE = math.log2(math.e) / math.sqrt(DH)
VMEM = pl.BlockSpec(memory_space=pltpu.VMEM)
SMEM = pl.BlockSpec(memory_space=pltpu.SMEM)
PARAMS = pltpu.CompilerParams(vmem_limit_bytes=40 * 2**20)


def swap(block, axis, distance):
    return lax.ppermute(
        block, axis, [(i, i ^ distance) for i in range(lax.axis_size(axis))]
    )


def attend_kernel(starts, limit, newpos, q, k, v, k_new, v_new, out, *, rows_each):
    rows, slots, fresh = q.shape[0], k.shape[0], k_new.shape[0]
    heads = q.shape[1] // DH
    bias = jnp.where(
        lax.broadcasted_iota(jnp.int32, (1, slots), 1) < limit[0], 0.0, MASKED
    ).astype(jnp.float32)
    in_block = lax.broadcasted_iota(jnp.int32, (rows_each, fresh), 0)
    positions = jnp.concatenate(
        [in_block + starts[b] for b in range(rows // rows_each)], axis=0
    )
    visible = newpos[...] <= positions
    lane = lax.broadcasted_iota(jnp.int32, (rows, DH), 1)
    stats = jnp.zeros((rows, DH), jnp.float32)
    ones = jnp.ones((slots, DH), jnp.bfloat16)
    ones_new = jnp.ones((fresh, DH), jnp.bfloat16)
    across = (((1,), (1,)), ((), ()))
    for h in range(heads):
        cols = slice(h * DH, (h + 1) * DH)
        queries = q[:, cols]
        scores = lax.dot_general(queries, k[:, cols], across, preferred_element_type=jnp.float32)
        scores = scores + bias
        scores_new = lax.dot_general(
            queries, k_new[:, cols], across, preferred_element_type=jnp.float32
        )
        scores_new = jnp.where(visible, scores_new, MASKED)
        top = jnp.maximum(
            jnp.max(scores, axis=1, keepdims=True), jnp.max(scores_new, axis=1, keepdims=True)
        )
        top = top.astype(jnp.bfloat16).astype(jnp.float32)
        weights = jnp.exp2((scores - top) * EXP2_SCALE).astype(jnp.bfloat16)
        weights_new = jnp.exp2((scores_new - top) * EXP2_SCALE).astype(jnp.bfloat16)
        both = jnp.dot(
            weights,
            jnp.concatenate([v[:, cols], ones], axis=1),
            preferred_element_type=jnp.float32,
        ) + jnp.dot(
            weights_new,
            jnp.concatenate([v_new[:, cols], ones_new], axis=1),
            preferred_element_type=jnp.float32,
        )
        out[:, cols] = both[:, :DH].astype(jnp.bfloat16)
        total = both[:, DH:]
        coarse = total.astype(jnp.bfloat16).astype(jnp.float32)
        stats = jnp.where(lane == h, top, stats)
        stats = jnp.where(lane == heads + h, coarse, stats)
        stats = jnp.where(lane == 2 * heads + h, total - coarse, stats)
    out[:, heads * DH :] = stats.astype(jnp.bfloat16)


def attend(starts, limit, newpos, q, k, v, k_new, v_new, rows_each):
    rows, width = q.shape
    keys = k.shape[0] + k_new.shape[0]
    return pl.pallas_call(
        functools.partial(attend_kernel, rows_each=rows_each),
        out_shape=jax.ShapeDtypeStruct((rows, width + DH), jnp.bfloat16),
        in_specs=[SMEM, SMEM] + [VMEM] * 6,
        out_specs=VMEM,
        compiler_params=PARAMS,
        cost_estimate=pl.CostEstimate(
            flops=4 * rows * keys * width,
            bytes_accessed=4 * keys * width + 4 * rows * width,
            transcendentals=rows * keys * width // DH,
        ),
        name="attend",
    )(starts, limit, newpos, q, k, v, k_new, v_new)


def combine_kernel(*refs, final):
    parts, out = refs[:-1], refs[-1]
    rows, heads = out.shape[0], (parts[0].shape[1] - DH) // DH
    stats = [p[:, heads * DH :].astype(jnp.float32) for p in parts]
    top = functools.reduce(jnp.maximum, [s[:, :heads] for s in stats])
    factors = [jnp.exp2((s[:, :heads] - top) * EXP2_SCALE) for s in stats]
    total = sum(
        f * (s[:, heads : 2 * heads] + s[:, 2 * heads : 3 * heads])
        for f, s in zip(factors, stats)
    )
    if final:
        factors = [f / total for f in factors]
    for h in range(heads):
        cols = slice(h * DH, (h + 1) * DH)
        mixed = sum(
            p[:, cols].astype(jnp.float32) * f[:, h : h + 1] for p, f in zip(parts, factors)
        )
        out[:, cols] = mixed.astype(jnp.bfloat16)
    if not final:
        coarse = total.astype(jnp.bfloat16).astype(jnp.float32)
        rest = jnp.zeros((rows, DH - 3 * heads), jnp.float32)
        out[:, heads * DH :] = jnp.concatenate(
            [top, coarse, total - coarse, rest], axis=1
        ).astype(jnp.bfloat16)


def combine(parts, final):
    rows, width = parts[0].shape
    out_width = width - DH if final else width
    return pl.pallas_call(
        functools.partial(combine_kernel, final=final),
        out_shape=jax.ShapeDtypeStruct((rows, out_width), jnp.bfloat16),
        in_specs=[VMEM] * len(parts),
        out_specs=VMEM,
        compiler_params=PARAMS,
        cost_estimate=pl.CostEstimate(
            flops=4 * len(parts) * rows * width,
            bytes_accessed=2 * (len(parts) + 1) * rows * width,
            transcendentals=rows * 8,
        ),
        name="combine",
    )(*parts)


def body(
    q_new,
    k_new,
    v_new,
    cache_k,
    cache_v,
    filled_slots,
    norm_gain,
    v_branch,
    x_gate,
    conv_state,
    conv_filter,
    skip_gain,
):
    ctx_size, uly_size = lax.axis_size("ctx"), lax.axis_size("uly")
    ctx, uly = lax.axis_index("ctx"), lax.axis_index("uly")
    tokens = q_new.shape[0]
    slots = cache_k.shape[0]
    bits = [1 << b for b in reversed(range(uly_size.bit_length() - 1))]

    def to_heads(block):
        for bit in bits:
            half = block.shape[1] // 2
            left, right = block[:, :half], block[:, half:]
            low = (uly & bit) == 0
            kept, sent = jnp.where(low, left, right), jnp.where(low, right, left)
            block = jnp.concatenate([kept, swap(sent, "uly", bit)], axis=0)
        return block

    def to_tokens(block):
        for bit in reversed(bits):
            half = block.shape[0] // 2
            kept, received = block[:half], swap(block[half:], "uly", bit)
            low = (uly & bit) == 0
            block = jnp.concatenate(
                [jnp.where(low, kept, received), jnp.where(low, received, kept)], axis=1
            )
        return block

    offsets = [0]
    for bit in bits:
        offsets = offsets + [o | bit for o in offsets]
    owners = uly ^ jnp.array(offsets, jnp.int32)

    def starts_of(distance):
        return ((ctx ^ distance) * uly_size + owners) * tokens

    limit = jnp.clip(filled_slots - ctx * slots, 0, slots).astype(jnp.int32)
    newpos = (starts_of(0)[:, None] + jnp.arange(tokens, dtype=jnp.int32)[None, :]).reshape(1, -1)

    here = to_heads(q_new)
    fresh = to_heads(jnp.concatenate([k_new, v_new], axis=0))
    fresh = fresh.reshape(uly_size, 2, tokens, -1)
    fresh_k = fresh[:, 0].reshape(here.shape)
    fresh_v = fresh[:, 1].reshape(here.shape)

    distances = list(range(2, ctx_size, 2))[::-1] + [0]
    mine = [swap(here, "ctx", d) if d else here for d in distances]
    other = [swap(block, "ctx", 1) for block in mine]

    def run(blocks, block_distances):
        starts = jnp.concatenate([starts_of(d) for d in block_distances])
        return attend(
            starts,
            limit,
            newpos,
            jnp.concatenate(blocks, axis=0),
            cache_k,
            cache_v,
            fresh_k,
            fresh_v,
            tokens,
        )

    rows = here.shape[0]
    other_distances = [d ^ 1 for d in distances]
    half = len(distances) // 2
    out_mine = run(mine, distances)
    returned = []
    for part in (slice(0, half), slice(half, None)):
        out_other = run(other[part], other_distances[part])
        back = swap(out_other, "ctx", 1)
        first = part.start * rows
        merged = combine([out_mine[first : first + back.shape[0]], back], False)
        for i, d in enumerate(distances[part]):
            piece = merged[i * rows : (i + 1) * rows]
            returned.append(swap(piece, "ctx", d) if d else piece)
    attended = combine(returned, True)
    token_rows = to_tokens(attended)

    values32 = token_rows.astype(jnp.float32)
    normed = (
        values32
        * lax.rsqrt(jnp.mean(values32 * values32, axis=1, keepdims=True) + 1e-06)
        * norm_gain
    )
    conv_input = lax.optimization_barrier(
        (normed * v_branch.astype(jnp.float32)).astype(jnp.bfloat16)
    )
    conv_reach = conv_filter.shape[0] - 1
    axes = ("ctx", "uly")
    count = ctx_size * uly_size
    incoming = lax.ppermute(conv_input[-conv_reach:], axes, [(i, i + 1) for i in range(count - 1)])
    first_device = jnp.logical_and(ctx == 0, uly == 0)
    lower_rim = jnp.where(first_device, conv_state, incoming)
    extended = jnp.concatenate([lower_rim, conv_input], axis=0).astype(jnp.float32)
    tap_table = jnp.repeat(conv_filter, conv_input.shape[1] // conv_filter.shape[1], axis=1)
    filtered = tap_table[0] * extended[conv_reach : conv_reach + tokens]
    for lag in range(1, conv_reach + 1):
        filtered = filtered + tap_table[lag] * extended[conv_reach - lag : conv_reach - lag + tokens]
    result = x_gate.astype(jnp.float32) * (filtered + skip_gain * conv_input.astype(jnp.float32))
    return result.astype(jnp.bfloat16)


def solution(mesh):
    split = P(("ctx", "uly"), None)
    in_specs = (
        split, split, split, P("ctx", "uly"), P("ctx", "uly"), P(),
        P(), split, split, P(), P(), P(),
    )
    return jax.shard_map(body, mesh=mesh, in_specs=in_specs, out_specs=split, check_vma=False)
```

```python
import functools
import math

import jax
import jax.numpy as jnp
from jax import lax
from jax.experimental import pallas as pl
from jax.experimental.pallas import tpu as pltpu
from jax.sharding import PartitionSpec as P

DH = 128
MASKED = -(2.0**100)
EXP2_SCALE = math.log2(math.e) / math.sqrt(DH)
VMEM = pl.BlockSpec(memory_space=pltpu.VMEM)
SMEM = pl.BlockSpec(memory_space=pltpu.SMEM)
PARAMS = pltpu.CompilerParams(vmem_limit_bytes=40 * 2**20)


def swap(block, axis, distance):
    return lax.ppermute(
        block, axis, [(i, i ^ distance) for i in range(lax.axis_size(axis))]
    )


def after(block, *earlier):
    return lax.optimization_barrier((block, *earlier))[0]


def attend_kernel(starts, limit, newpos, q, k, v, k_new, v_new, out, *, rows_each):
    rows, slots, fresh = q.shape[0], k.shape[0], k_new.shape[0]
    heads = q.shape[1] // DH
    bias = jnp.where(
        lax.broadcasted_iota(jnp.int32, (1, slots), 1) < limit[0], 0.0, MASKED
    ).astype(jnp.float32)
    in_block = lax.broadcasted_iota(jnp.int32, (rows_each, fresh), 0)
    positions = jnp.concatenate(
        [in_block + starts[b] for b in range(rows // rows_each)], axis=0
    )
    visible = newpos[...] <= positions
    lane = lax.broadcasted_iota(jnp.int32, (rows, DH), 1)
    stats = jnp.zeros((rows, DH), jnp.float32)
    ones = jnp.ones((slots, DH), jnp.bfloat16)
    ones_new = jnp.ones((fresh, DH), jnp.bfloat16)
    across = (((1,), (1,)), ((), ()))
    def score(h):
        cols = slice(h * DH, (h + 1) * DH)
        queries = q[:, cols]
        scores = lax.dot_general(queries, k[:, cols], across, preferred_element_type=jnp.float32)
        scores_new = lax.dot_general(
            queries, k_new[:, cols], across, preferred_element_type=jnp.float32
        )
        return scores + bias, jnp.where(visible, scores_new, MASKED)

    def weigh_keys(scores, scores_new):
        top = jnp.maximum(
            jnp.max(scores, axis=1, keepdims=True), jnp.max(scores_new, axis=1, keepdims=True)
        )
        top = top.astype(jnp.bfloat16).astype(jnp.float32)
        weights = jnp.exp2((scores - top) * EXP2_SCALE).astype(jnp.bfloat16)
        weights_new = jnp.exp2((scores_new - top) * EXP2_SCALE).astype(jnp.bfloat16)
        return top, weights, weights_new

    def apply_values(h, stats, top, weights, weights_new):
        cols = slice(h * DH, (h + 1) * DH)
        both = jnp.dot(
            weights,
            jnp.concatenate([v[:, cols], ones], axis=1),
            preferred_element_type=jnp.float32,
        ) + jnp.dot(
            weights_new,
            jnp.concatenate([v_new[:, cols], ones_new], axis=1),
            preferred_element_type=jnp.float32,
        )
        out[:, cols] = both[:, :DH].astype(jnp.bfloat16)
        total = both[:, DH:]
        coarse = total.astype(jnp.bfloat16).astype(jnp.float32)
        stats = jnp.where(lane == h, top, stats)
        stats = jnp.where(lane == heads + h, coarse, stats)
        return jnp.where(lane == 2 * heads + h, total - coarse, stats)

    scored = [score(h) for h in range(heads)]
    weighed = [weigh_keys(*pair) for pair in scored]
    for h in range(heads):
        stats = apply_values(h, stats, *weighed[h])
    out[:, heads * DH :] = stats.astype(jnp.bfloat16)


def attend(starts, limit, newpos, q, k, v, k_new, v_new, rows_each):
    rows, width = q.shape
    keys = k.shape[0] + k_new.shape[0]
    return pl.pallas_call(
        functools.partial(attend_kernel, rows_each=rows_each),
        out_shape=jax.ShapeDtypeStruct((rows, width + DH), jnp.bfloat16),
        in_specs=[SMEM, SMEM] + [VMEM] * 6,
        out_specs=VMEM,
        compiler_params=PARAMS,
        cost_estimate=pl.CostEstimate(
            flops=4 * rows * keys * width,
            bytes_accessed=4 * keys * width + 4 * rows * width,
            transcendentals=rows * keys * width // DH,
        ),
        name="attend",
    )(starts, limit, newpos, q, k, v, k_new, v_new)


def prepare_kernel(place, k, v, kept, sent, *, chips):
    tokens, width = k.shape[0], kept.shape[1]
    chip, core = place[0], place[1]
    for n in range(chips):
        group = (chip ^ n) * 2
        mine = pl.ds(pl.multiple_of((group + core) * width, DH), width)
        his = pl.ds(pl.multiple_of((group + 1 - core) * width, DH), width)
        for i, ref in enumerate((k, v)):
            rows = slice((2 * n + i) * tokens, (2 * n + i + 1) * tokens)
            kept[rows, :] = ref[:, mine]
            sent[rows, :] = ref[:, his]


def prepare(place, k, v, chips, width):
    tokens = k.shape[0]
    shape = jax.ShapeDtypeStruct((chips * 2 * tokens, width), k.dtype)
    return pl.pallas_call(
        functools.partial(prepare_kernel, chips=chips),
        out_shape=[shape, shape],
        in_specs=[SMEM] + [VMEM] * 2,
        out_specs=[VMEM, VMEM],
        compiler_params=PARAMS,
        cost_estimate=pl.CostEstimate(flops=0, bytes_accessed=8 * k.size, transcendentals=0),
        name="prepare",
    )(place, k, v)


def weigh(blocks, heads):
    stats = [b[:, heads * DH :].astype(jnp.float32) for b in blocks]
    top = functools.reduce(jnp.maximum, [s[:, :heads] for s in stats])
    factors = [jnp.exp2((s[:, :heads] - top) * EXP2_SCALE) for s in stats]
    total = sum(
        f * (s[:, heads : 2 * heads] + s[:, 2 * heads : 3 * heads])
        for f, s in zip(factors, stats)
    )
    return top, factors, total


def mix(blocks, factors, h):
    cols = slice(h * DH, (h + 1) * DH)
    return sum(b[:, cols].astype(jnp.float32) * f[:, h : h + 1] for b, f in zip(blocks, factors))


def merge_kernel(*refs, sides, nears, count):
    parts, outs = refs[: sides * nears], refs[sides * nears :]
    heads = (parts[0].shape[1] - DH) // DH
    rows = parts[0].shape[0]
    for n in range(nears):
        blocks = [parts[side * nears + n] for side in range(sides)]
        top, factors, total = weigh(blocks, heads)
        coarse = total.astype(jnp.bfloat16).astype(jnp.float32)
        rest = jnp.zeros((rows, DH - 3 * heads), jnp.float32)
        stats = jnp.concatenate([top, coarse, total - coarse, rest], axis=1).astype(jnp.bfloat16)
        pieces = [mix(blocks, factors, h).astype(jnp.bfloat16) for h in range(heads)]
        for i in range(len(outs)):
            source, target = slice(i * count, (i + 1) * count), slice(n * count, (n + 1) * count)
            for h in range(heads):
                outs[i][target, h * DH : (h + 1) * DH] = pieces[h][source]
            outs[i][target, heads * DH :] = stats[source]


def merge(parts, sides, nears, count):
    rows, width = parts[0].shape
    shape = jax.ShapeDtypeStruct((nears * count, width), jnp.bfloat16)
    return pl.pallas_call(
        functools.partial(merge_kernel, sides=sides, nears=nears, count=count),
        out_shape=[shape] * (rows // count),
        in_specs=[VMEM] * len(parts),
        out_specs=[VMEM] * (rows // count),
        compiler_params=PARAMS,
        cost_estimate=pl.CostEstimate(
            flops=4 * len(parts) * rows * width,
            bytes_accessed=4 * len(parts) * rows * width,
            transcendentals=rows * 8,
        ),
        name="merge",
    )(*parts)


def finish_kernel(*refs):
    parts, out = refs[:-1], refs[-1]
    heads = out.shape[1] // DH
    _, factors, total = weigh(parts, heads)
    factors = [f / total for f in factors]
    for h in range(heads):
        out[:, h * DH : (h + 1) * DH] = mix(parts, factors, h).astype(jnp.bfloat16)


def finish(parts):
    rows, width = parts[0].shape
    return pl.pallas_call(
        finish_kernel,
        out_shape=jax.ShapeDtypeStruct((rows, width - DH), jnp.bfloat16),
        in_specs=[VMEM] * len(parts),
        out_specs=VMEM,
        compiler_params=PARAMS,
        cost_estimate=pl.CostEstimate(
            flops=4 * len(parts) * rows * width,
            bytes_accessed=2 * (len(parts) + 1) * rows * width,
            transcendentals=rows * 8,
        ),
        name="finish",
    )(*parts)


def body(
    q_new,
    k_new,
    v_new,
    cache_k,
    cache_v,
    filled_slots,
    norm_gain,
    v_branch,
    x_gate,
    conv_state,
    conv_filter,
    skip_gain,
):
    ctx_size, uly_size = lax.axis_size("ctx"), lax.axis_size("uly")
    ctx, uly = lax.axis_index("ctx"), lax.axis_index("uly")
    chip, core, chips = uly // 2, uly % 2, uly_size // 2
    tokens, channels = q_new.shape
    slots, width = cache_k.shape
    pair = 2 * tokens
    axes = ("ctx", "uly")
    count = ctx_size * uly_size
    places = [(side, near) for side in range(2) for near in range(chips)]

    def route(block, side, near):
        if side == 0 and near == 0:
            return block
        flip = side * uly_size + 2 * near
        return lax.ppermute(block, axes, [(i, i ^ flip) for i in range(count)])

    def starts_of(far, side, near):
        owner = (ctx ^ (far + side)) * uly_size + (uly ^ jnp.arange(2 * near, 2 * near + 2))
        return (owner * tokens).astype(jnp.int32)

    limit = jnp.clip(filled_slots - ctx * slots, 0, slots).astype(jnp.int32)
    newpos = jnp.concatenate([starts_of(0, 0, n) for n in range(chips)])
    newpos = (newpos[:, None] + jnp.arange(tokens, dtype=jnp.int32)[None, :]).reshape(1, -1)

    place = jnp.stack([chip, core]).astype(jnp.int32)

    def columns(block, near, half):
        return lax.dynamic_slice_in_dim(block, ((chip ^ near) * 2 + half) * width, width, 1)

    sent = jnp.concatenate([columns(q_new, n, 1 - core) for n in range(chips)], axis=0)
    received = swap(sent, "uly", 1)
    here = jnp.concatenate(
        [
            part
            for n in range(chips)
            for part in (columns(q_new, n, core), received[n * tokens : (n + 1) * tokens])
        ],
        axis=0,
    )
    blocks = {0: here}
    for far in [2, *range(ctx_size - 2, 2, -2)]:
        blocks[far] = swap(here, "ctx", far)
    chunks = [[far, far + 2] for far in range(0, ctx_size, 4)]
    kept, sent = prepare(place, k_new, v_new, chips, width)
    pairs = [b.reshape(chips, pair, width) for b in (kept, swap(sent, "uly", 1))]
    fresh_parts = [jnp.concatenate([b[n] for b in pairs], axis=0) for n in range(chips)]
    spread, fresh = [], [fresh_parts[0]]
    for i, chunk in enumerate(chunks):
        sent = [
            jnp.concatenate([blocks[far][n * pair : (n + 1) * pair] for far in chunk], axis=0)
            for n in range(chips)
        ]
        if i:
            sent = [after(block, spread[i - 1][1, 0]) for block in sent]
        got = {}
        for side, n in places:
            if i == 0 and side == 0 and n:
                whole = route(jnp.concatenate([sent[n], fresh_parts[n]], axis=0), side, n)
                got[side, n] = whole[: len(chunk) * pair]
                fresh.append(whole[len(chunk) * pair :])
            else:
                got[side, n] = route(sent[n], side, n)
        spread.append(got)
    fresh = jnp.concatenate(fresh, axis=0).reshape(uly_size, 2, tokens, width)
    fresh_k = fresh[:, 0].reshape(uly_size * tokens, width)
    fresh_v = fresh[:, 1].reshape(uly_size * tokens, width)

    def run(chunk, queries):
        rows = len(chunk) * pair
        out = attend(
            jnp.concatenate([starts_of(far, *p) for p in places for far in chunk]),
            limit,
            newpos,
            jnp.concatenate([queries[p] for p in places], axis=0),
            cache_k,
            cache_v,
            fresh_k,
            fresh_v,
            tokens,
        )
        return {p: out[i * rows : (i + 1) * rows] for i, p in enumerate(places)}

    outs = []
    for chunk, queries in zip(chunks, spread):
        if outs:
            queries = {p: after(block, outs[-1][0, 0]) for p, block in queries.items()}
        outs.append(run(chunk, queries))
    merged = {}
    for chunk, out in zip(chunks[::-1], outs[::-1]):
        got = [route(out[p], *p) for p in places]
        merged |= zip(chunk, merge(got, 2, chips, pair))
    final = [merged[0]]
    for far in sorted(merged)[:0:-1]:
        final.append(swap(merged[far], "ctx", far))
    attended = finish(final).reshape(chips, 2, tokens, width)
    sibling = swap(attended[:, 1], "uly", 1)
    both = jnp.stack([attended[:, 0], sibling])
    token_rows = jnp.concatenate(
        [
            lax.dynamic_slice(both, (half ^ core, group ^ chip, 0, 0), (1, 1, tokens, width))[0, 0]
            for group in range(chips)
            for half in range(2)
        ],
        axis=1,
    )
    values32 = token_rows.astype(jnp.float32)
    normed = (
        values32
        * lax.rsqrt(jnp.mean(values32 * values32, axis=1, keepdims=True) + 1e-06)
        * norm_gain
    )
    conv_input = lax.optimization_barrier(
        (normed * v_branch.astype(jnp.float32)).astype(jnp.bfloat16)
    )
    conv_reach = conv_filter.shape[0] - 1
    incoming = lax.ppermute(conv_input[-conv_reach:], axes, [(i, i + 1) for i in range(count - 1)])
    first_device = jnp.logical_and(ctx == 0, uly == 0)
    lower_rim = jnp.where(first_device, conv_state, incoming)
    extended = jnp.concatenate([lower_rim, conv_input], axis=0).astype(jnp.float32)
    tap_table = jnp.repeat(conv_filter, conv_input.shape[1] // conv_filter.shape[1], axis=1)
    filtered = tap_table[0] * extended[conv_reach : conv_reach + tokens]
    for lag in range(1, conv_reach + 1):
        filtered = filtered + tap_table[lag] * extended[conv_reach - lag : conv_reach - lag + tokens]
    result = x_gate.astype(jnp.float32) * (filtered + skip_gain * conv_input.astype(jnp.float32))
    return result.astype(jnp.bfloat16)


def solution(mesh):
    split = P(("ctx", "uly"), None)
    in_specs = (
        split, split, split, P("ctx", "uly"), P("ctx", "uly"), P(),
        P(), split, split, P(), P(), P(),
    )
    return jax.shard_map(body, mesh=mesh, in_specs=in_specs, out_specs=split, check_vma=False)
```

```python
import functools
import math

import jax
import jax.numpy as jnp
from jax import lax
from jax.experimental import pallas as pl
from jax.experimental.pallas import tpu as pltpu
from jax.sharding import PartitionSpec as P

DH = 128
MASKED = -(2.0**100)
EXP2_SCALE = math.log2(math.e) / math.sqrt(DH)
VMEM = pl.BlockSpec(memory_space=pltpu.VMEM)
SMEM = pl.BlockSpec(memory_space=pltpu.SMEM)
PARAMS = pltpu.CompilerParams(vmem_limit_bytes=40 * 2**20)


def swap(block, axis, distance):
    return lax.ppermute(
        block, axis, [(i, i ^ distance) for i in range(lax.axis_size(axis))]
    )


def after(block, *earlier):
    return lax.optimization_barrier((block, *earlier))[0]


def attend_kernel(starts, limit, newpos, q, k, v, k_new, v_new, out, *, rows_each):
    rows, slots, fresh = q.shape[0], k.shape[0], k_new.shape[0]
    heads = q.shape[1] // DH
    bias = jnp.where(
        lax.broadcasted_iota(jnp.int32, (1, slots), 1) < limit[0], 0.0, MASKED
    ).astype(jnp.float32)
    in_block = lax.broadcasted_iota(jnp.int32, (rows_each, fresh), 0)
    positions = jnp.concatenate(
        [in_block + starts[b] for b in range(rows // rows_each)], axis=0
    )
    visible = newpos[...] <= positions
    lane = lax.broadcasted_iota(jnp.int32, (rows, DH), 1)
    stats = jnp.zeros((rows, DH), jnp.float32)
    ones = jnp.ones((slots, DH), jnp.bfloat16)
    ones_new = jnp.ones((fresh, DH), jnp.bfloat16)
    across = (((1,), (1,)), ((), ()))
    def score(h):
        cols = slice(h * DH, (h + 1) * DH)
        queries = q[:, cols]
        scores = lax.dot_general(queries, k[:, cols], across, preferred_element_type=jnp.float32)
        scores_new = lax.dot_general(
            queries, k_new[:, cols], across, preferred_element_type=jnp.float32
        )
        return scores + bias, jnp.where(visible, scores_new, MASKED)

    def weigh_keys(scores, scores_new):
        top = jnp.maximum(
            jnp.max(scores, axis=1, keepdims=True), jnp.max(scores_new, axis=1, keepdims=True)
        )
        top = top.astype(jnp.bfloat16).astype(jnp.float32)
        weights = jnp.exp2((scores - top) * EXP2_SCALE).astype(jnp.bfloat16)
        weights_new = jnp.exp2((scores_new - top) * EXP2_SCALE).astype(jnp.bfloat16)
        return top, weights, weights_new

    def apply_values(h, stats, top, weights, weights_new):
        cols = slice(h * DH, (h + 1) * DH)
        both = jnp.dot(
            weights,
            jnp.concatenate([v[:, cols], ones], axis=1),
            preferred_element_type=jnp.float32,
        ) + jnp.dot(
            weights_new,
            jnp.concatenate([v_new[:, cols], ones_new], axis=1),
            preferred_element_type=jnp.float32,
        )
        out[:, cols] = both[:, :DH].astype(jnp.bfloat16)
        total = both[:, DH:]
        coarse = total.astype(jnp.bfloat16).astype(jnp.float32)
        stats = jnp.where(lane == h, top, stats)
        stats = jnp.where(lane == heads + h, coarse, stats)
        return jnp.where(lane == 2 * heads + h, total - coarse, stats)

    scored = [score(h) for h in range(heads)]
    weighed = [weigh_keys(*pair) for pair in scored]
    for h in range(heads):
        stats = apply_values(h, stats, *weighed[h])
    out[:, heads * DH :] = stats.astype(jnp.bfloat16)


def attend(starts, limit, newpos, q, k, v, k_new, v_new, rows_each):
    rows, width = q.shape
    keys = k.shape[0] + k_new.shape[0]
    return pl.pallas_call(
        functools.partial(attend_kernel, rows_each=rows_each),
        out_shape=jax.ShapeDtypeStruct((rows, width + DH), jnp.bfloat16),
        in_specs=[SMEM, SMEM] + [VMEM] * 6,
        out_specs=VMEM,
        compiler_params=PARAMS,
        cost_estimate=pl.CostEstimate(
            flops=4 * rows * keys * width,
            bytes_accessed=4 * keys * width + 4 * rows * width,
            transcendentals=rows * keys * width // DH,
        ),
        name="attend",
    )(starts, limit, newpos, q, k, v, k_new, v_new)


def prepare_kernel(place, k, v, kept, sent, *, chips):
    tokens, width = k.shape[0], kept.shape[1]
    chip, core = place[0], place[1]
    for n in range(chips):
        group = (chip ^ n) * 2
        mine = pl.ds(pl.multiple_of((group + core) * width, DH), width)
        his = pl.ds(pl.multiple_of((group + 1 - core) * width, DH), width)
        for i, ref in enumerate((k, v)):
            rows = slice((2 * n + i) * tokens, (2 * n + i + 1) * tokens)
            kept[rows, :] = ref[:, mine]
            sent[rows, :] = ref[:, his]


def prepare(place, k, v, chips, width):
    tokens = k.shape[0]
    shape = jax.ShapeDtypeStruct((chips * 2 * tokens, width), k.dtype)
    return pl.pallas_call(
        functools.partial(prepare_kernel, chips=chips),
        out_shape=[shape, shape],
        in_specs=[SMEM] + [VMEM] * 2,
        out_specs=[VMEM, VMEM],
        compiler_params=PARAMS,
        cost_estimate=pl.CostEstimate(flops=0, bytes_accessed=8 * k.size, transcendentals=0),
        name="prepare",
    )(place, k, v)


def weigh(blocks, heads):
    stats = [b[:, heads * DH :].astype(jnp.float32) for b in blocks]
    top = functools.reduce(jnp.maximum, [s[:, :heads] for s in stats])
    factors = [jnp.exp2((s[:, :heads] - top) * EXP2_SCALE) for s in stats]
    total = sum(
        f * (s[:, heads : 2 * heads] + s[:, 2 * heads : 3 * heads])
        for f, s in zip(factors, stats)
    )
    return top, factors, total


def mix(blocks, factors, h):
    cols = slice(h * DH, (h + 1) * DH)
    return sum(b[:, cols].astype(jnp.float32) * f[:, h : h + 1] for b, f in zip(blocks, factors))


def merge_kernel(*refs, sides, nears, count):
    parts, outs = refs[: sides * nears], refs[sides * nears :]
    heads = (parts[0].shape[1] - DH) // DH
    rows = parts[0].shape[0]
    blocks = [
        jnp.concatenate([parts[side * nears + n][...] for n in range(nears)], axis=0)
        for side in range(sides)
    ]
    top, factors, total = weigh(blocks, heads)
    coarse = total.astype(jnp.bfloat16).astype(jnp.float32)
    rest = jnp.zeros((nears * rows, DH - 3 * heads), jnp.float32)
    stats = jnp.concatenate([top, coarse, total - coarse, rest], axis=1).astype(jnp.bfloat16)
    for h in range(heads + 1):
        piece = mix(blocks, factors, h).astype(jnp.bfloat16) if h < heads else stats
        for i, out in enumerate(outs):
            for n in range(nears):
                first = n * rows + i * count
                out[n * count : (n + 1) * count, h * DH : (h + 1) * DH] = piece[first : first + count]


def merge(parts, sides, nears, count):
    rows, width = parts[0].shape
    shape = jax.ShapeDtypeStruct((nears * count, width), jnp.bfloat16)
    return pl.pallas_call(
        functools.partial(merge_kernel, sides=sides, nears=nears, count=count),
        out_shape=[shape] * (rows // count),
        in_specs=[VMEM] * len(parts),
        out_specs=[VMEM] * (rows // count),
        compiler_params=PARAMS,
        cost_estimate=pl.CostEstimate(
            flops=4 * len(parts) * rows * width,
            bytes_accessed=4 * len(parts) * rows * width,
            transcendentals=rows * 8,
        ),
        name="merge",
    )(*parts)


def finish_kernel(*refs):
    parts, out = refs[:-1], refs[-1]
    heads = out.shape[1] // DH
    _, factors, total = weigh(parts, heads)
    factors = [f / total for f in factors]
    for h in range(heads):
        out[:, h * DH : (h + 1) * DH] = mix(parts, factors, h).astype(jnp.bfloat16)


def finish(parts):
    rows, width = parts[0].shape
    return pl.pallas_call(
        finish_kernel,
        out_shape=jax.ShapeDtypeStruct((rows, width - DH), jnp.bfloat16),
        in_specs=[VMEM] * len(parts),
        out_specs=VMEM,
        compiler_params=PARAMS,
        cost_estimate=pl.CostEstimate(
            flops=4 * len(parts) * rows * width,
            bytes_accessed=2 * (len(parts) + 1) * rows * width,
            transcendentals=rows * 8,
        ),
        name="finish",
    )(*parts)


def body(
    q_new,
    k_new,
    v_new,
    cache_k,
    cache_v,
    filled_slots,
    norm_gain,
    v_branch,
    x_gate,
    conv_state,
    conv_filter,
    skip_gain,
):
    ctx_size, uly_size = lax.axis_size("ctx"), lax.axis_size("uly")
    ctx, uly = lax.axis_index("ctx"), lax.axis_index("uly")
    chip, core, chips = uly // 2, uly % 2, uly_size // 2
    tokens, channels = q_new.shape
    slots, width = cache_k.shape
    pair = 2 * tokens
    axes = ("ctx", "uly")
    count = ctx_size * uly_size
    places = [(side, near) for side in range(2) for near in range(chips)]

    def route(block, side, near):
        if side == 0 and near == 0:
            return block
        flip = side * uly_size + 2 * near
        return lax.ppermute(block, axes, [(i, i ^ flip) for i in range(count)])

    def starts_of(far, side, near):
        owner = (ctx ^ (far + side)) * uly_size + (uly ^ jnp.arange(2 * near, 2 * near + 2))
        return (owner * tokens).astype(jnp.int32)

    limit = jnp.clip(filled_slots - ctx * slots, 0, slots).astype(jnp.int32)
    newpos = jnp.concatenate([starts_of(0, 0, n) for n in range(chips)])
    newpos = (newpos[:, None] + jnp.arange(tokens, dtype=jnp.int32)[None, :]).reshape(1, -1)

    place = jnp.stack([chip, core]).astype(jnp.int32)

    def columns(block, near, half):
        return lax.dynamic_slice_in_dim(block, ((chip ^ near) * 2 + half) * width, width, 1)

    sent = jnp.concatenate([columns(q_new, n, 1 - core) for n in range(chips)], axis=0)
    received = swap(sent, "uly", 1)
    here = jnp.concatenate(
        [
            part
            for n in range(chips)
            for part in (columns(q_new, n, core), received[n * tokens : (n + 1) * tokens])
        ],
        axis=0,
    )
    blocks = {0: here}
    for far in range(2, ctx_size, 2):
        blocks[far] = swap(here, "ctx", far)
    chunks = [[far, far + 2] for far in range(0, ctx_size, 4)]
    kept, sent = prepare(place, k_new, v_new, chips, width)
    pairs = [b.reshape(chips, pair, width) for b in (kept, swap(sent, "uly", 1))]
    fresh_parts = [jnp.concatenate([b[n] for b in pairs], axis=0) for n in range(chips)]
    spread, fresh = [], [fresh_parts[0]]
    for i, chunk in enumerate(chunks):
        sent = [
            jnp.concatenate([blocks[far][n * pair : (n + 1) * pair] for far in chunk], axis=0)
            for n in range(chips)
        ]
        if i:
            sent = [after(block, spread[i - 1][1, 0]) for block in sent]
        got = {}
        for side, n in places:
            if i == 0 and side == 0 and n:
                whole = route(jnp.concatenate([sent[n], fresh_parts[n]], axis=0), side, n)
                got[side, n] = whole[: len(chunk) * pair]
                fresh.append(whole[len(chunk) * pair :])
            else:
                got[side, n] = route(sent[n], side, n)
        spread.append(got)
    fresh = jnp.concatenate(fresh, axis=0).reshape(uly_size, 2, tokens, width)
    fresh_k = fresh[:, 0].reshape(uly_size * tokens, width)
    fresh_v = fresh[:, 1].reshape(uly_size * tokens, width)

    def run(chunk, queries):
        rows = len(chunk) * pair
        out = attend(
            jnp.concatenate([starts_of(far, *p) for p in places for far in chunk]),
            limit,
            newpos,
            jnp.concatenate([queries[p] for p in places], axis=0),
            cache_k,
            cache_v,
            fresh_k,
            fresh_v,
            tokens,
        )
        return {p: out[i * rows : (i + 1) * rows] for i, p in enumerate(places)}

    outs = []
    for chunk, queries in zip(chunks, spread):
        if outs:
            queries = {p: after(block, outs[-1][0, 0]) for p, block in queries.items()}
        outs.append(run(chunk, queries))
    merged = {}
    for chunk, out in zip(chunks[::-1], outs[::-1]):
        got = [route(out[p], *p) for p in places]
        merged |= zip(chunk, merge(got, 2, chips, pair))
    final = [merged[0]]
    for far in sorted(merged)[:0:-1]:
        final.append(swap(merged[far], "ctx", far))
    attended = finish(final).reshape(chips, 2, tokens, width)
    sibling = swap(attended[:, 1], "uly", 1)
    both = jnp.stack([attended[:, 0], sibling])
    token_rows = jnp.concatenate(
        [
            lax.dynamic_slice(both, (half ^ core, group ^ chip, 0, 0), (1, 1, tokens, width))[0, 0]
            for group in range(chips)
            for half in range(2)
        ],
        axis=1,
    )
    values32 = token_rows.astype(jnp.float32)
    normed = (
        values32
        * lax.rsqrt(jnp.mean(values32 * values32, axis=1, keepdims=True) + 1e-06)
        * norm_gain
    )
    conv_input = lax.optimization_barrier(
        (normed * v_branch.astype(jnp.float32)).astype(jnp.bfloat16)
    )
    conv_reach = conv_filter.shape[0] - 1
    incoming = lax.ppermute(conv_input[-conv_reach:], axes, [(i, i + 1) for i in range(count - 1)])
    first_device = jnp.logical_and(ctx == 0, uly == 0)
    lower_rim = jnp.where(first_device, conv_state, incoming)
    extended = jnp.concatenate([lower_rim, conv_input], axis=0).astype(jnp.float32)
    tap_table = jnp.repeat(conv_filter, conv_input.shape[1] // conv_filter.shape[1], axis=1)
    filtered = tap_table[0] * extended[conv_reach : conv_reach + tokens]
    for lag in range(1, conv_reach + 1):
        filtered = filtered + tap_table[lag] * extended[conv_reach - lag : conv_reach - lag + tokens]
    result = x_gate.astype(jnp.float32) * (filtered + skip_gain * conv_input.astype(jnp.float32))
    return result.astype(jnp.bfloat16)


def solution(mesh):
    split = P(("ctx", "uly"), None)
    in_specs = (
        split, split, split, P("ctx", "uly"), P("ctx", "uly"), P(),
        P(), split, split, P(), P(), P(),
    )
    return jax.shard_map(body, mesh=mesh, in_specs=in_specs, out_specs=split, check_vma=False)
```
